32 devices in a mesh: box: 8 (over y, x, core), grp: 4 (over z).
Axes of the slice: x: 2, y: 2, z: 4, core: 2. Of those that a mesh axis runs over, the one named last changes fastest.
Arguments:
- source: bfloat16 [5120, 32, 32], P(('box', 'grp')), may hold values from -6 to 6
- conductivity: bfloat16 [5120, 32, 32], P(('box', 'grp')), may hold values from 0.25 to 4
- new_owner: int32 [8, 4, 5, 1], P('box', 'grp'), may hold values from 0 to 3; in each aligned block of 5 rows (0 to 4, 5 to 9, ..., all dimensions but the last counted through in order) at most 3 rows name the same one
Outputs:
- correction: bfloat16 [8, 4, 4, 3, 32768], P('box', 'grp')
- coarse_residual: float32 [4, 40, 4096], P('grp')
The draws below stay inside these ranges and needn't reach their ends.
Inputs may be any that keep to these rules, and one draw needn't show every extreme that they name: `new_owner`: boxes move only within their box index; among the 5 boxes of one device at most 3 share a new owner, and in every draw some device gives exactly 3 boxes to one owner.
All inputs are finite; a program needn't handle non-finite values.
Results may differ from the reference program's by a relative error of at most 0.001.
Values may be sent and summed in bfloat16 or wider, within the bound.
A program may use at most 128 MiB of HBM per device.

```python
import math
import jax
import jax.numpy as jnp
import numpy as np
from jax import lax

BZ = 32
BY = 32
BX = 32
B_DEV = 5
CAP = 3
NZ = 5120
CELLS = 32768
RC = 4096
N_BOX = 8
N_GRP = 4
DEVICES = 32


def block_levels(rng, shape, shards, least, high):
    level = 1.0
    for dim, parts in shards:
        steps = jax.random.uniform(jax.random.fold_in(jax.random.fold_in(rng, 6), dim), (parts,), jnp.float32, least / len(shards), high / len(shards))
        level = level * jnp.repeat(jnp.exp(steps), shape[dim] // parts).reshape((-1,) + (1,) * (len(shape) - 1 - dim))
    return level


def routed_block(stream_key, own, number, rows, number_of, top, most, skew):
    ranking = jax.random.permutation(stream_key, number_of)
    packed, common = load_shares(number_of, rows * top, most, skew, True), load_shares(number_of, rows * top, most, skew, False)
    places = jnp.arange(number_of)

    def named(sizes, rotation):
        used = int((sizes > 0).sum())
        fixed = max(1, used // 4)
        passed = fixed + (places - fixed + rotation * (used - fixed)) % max(1, number_of - fixed)
        return jnp.zeros((number_of,), jnp.int32).at[ranking[jnp.where(places < fixed, places, passed)]].set(jnp.asarray(sizes, jnp.int32))

    sizes = jnp.where(number % 4 == 0, named(packed, number // 4), named(common, number - number // 4 - 1))
    mixed = jax.random.permutation(jax.random.fold_in(own, 3), number_of)
    donor, sink = mixed[0:number_of // 2 * 2:2], mixed[1:number_of // 2 * 2:2]
    room = jnp.minimum(sizes[donor] - 1, most - sizes[sink]) // 2
    room = jnp.where((donor == ranking[0]) | (sink == ranking[0]) | (sizes[sink] == 0), 0, jnp.maximum(room, 0))
    passed = jax.random.randint(jax.random.fold_in(own, 4), (number_of // 2,), 0, 1 << 20) % (room + 1)
    sizes = sizes.at[donor].add(-passed).at[sink].add(passed)
    items = jnp.searchsorted(jnp.cumsum(sizes), jnp.arange(rows * top), side="right").astype(jnp.int32)
    grid = items.reshape(top, rows).T
    grid = grid[jax.random.permutation(jax.random.fold_in(own, 1), rows)]
    rotation = jax.random.randint(jax.random.fold_in(own, 2), (rows, 1), 0, top)
    return jnp.take_along_axis(grid, (jnp.arange(top)[None, :] + rotation) % top, axis=1)


def load_shares(count, total, reach, lean, full):
    portions = [(1 << 20) // math.isqrt(grade ** lean) + 1 for grade in range(1, count + 1)]
    largest = reach if full else min(reach, max(-(-total // count), total * portions[0] // sum(portions)))
    least = 1 if total - largest >= count - 1 else 0
    counts, spare = [largest] + [least] * (count - 1), total - largest - least * (count - 1)
    while spare > 0:
        free = [i for i in range(1, count) if counts[i] < largest] or [i for i in range(1, count) if counts[i] < reach]
        pool, left = sum([portions[i] for i in free]), spare
        for i in free:
            addition = min(reach - counts[i], max(1, left * portions[i] // pool), spare)
            counts[i] = counts[i] + addition
            spare = spare - addition
    return np.array(counts)


def scatter_about(rng, dims, deviation, reach, shards=(), kind=jnp.bfloat16):
    loudness = block_levels(rng, dims, shards, -0.22, 0.18) if shards else 1.0
    array = jax.random.normal(rng, dims, jnp.float32) * deviation * loudness
    return jnp.minimum(jnp.maximum(array, -reach), reach).astype(kind)


def setup_inputs(seed: int = 0) -> dict:
    key_list = jax.random.split(jax.random.key(seed), 4)
    source = scatter_about(key_list[0], (NZ, BY, BX), 1.0, 6.0, ((0, 32),))
    conductivity = jnp.clip(jnp.exp(math.log(4.0) - 2.7725887 * jax.random.uniform(key_list[1], (NZ, BY, BX), jnp.float32) ** block_levels(key_list[1], (NZ, BY, BX), ((0, 32),), -0.2, 0.2)), 0.25, 4.0).astype(jnp.bfloat16)
    new_owner_keys = jax.random.split(jax.random.fold_in(key_list[2], 1), N_BOX * N_GRP * B_DEV // B_DEV)
    new_owner_turns = jax.random.permutation(jax.random.fold_in(key_list[2], 3), N_BOX * N_GRP * B_DEV // B_DEV)
    new_owner = jax.vmap(lambda own, number: routed_block(jax.random.fold_in(key_list[2], 2), own, number, B_DEV, N_GRP, 1, CAP, 2))(new_owner_keys, new_owner_turns).reshape((N_BOX, N_GRP, B_DEV, 1))
    return dict(source=source, conductivity=conductivity, new_owner=new_owner)


WEIGHT = 0.8


def shift_next(values_in, which):
    extent = values_in.shape[which]
    widths = [(0, 0)] * values_in.ndim
    widths[which] = (0, 1)
    return jnp.pad(lax.slice_in_dim(values_in, 1, extent, axis=which), widths)


def shift_prev(values_in, which):
    extent = values_in.shape[which]
    widths = [(0, 0)] * values_in.ndim
    widths[which] = (1, 0)
    return jnp.pad(lax.slice_in_dim(values_in, 0, extent - 1, axis=which), widths)


def smooth(source, conductivity):
    inside = conductivity > 0
    axes_list = (conductivity.ndim - 3, conductivity.ndim - 2, conductivity.ndim - 1)
    face_list = []
    diagonal = jnp.zeros_like(conductivity)
    for which in axes_list:
        after = shift_next(conductivity, which)
        face_fwd = jnp.where(inside & (after > 0), 0.5 * (conductivity + after), 0.0)
        face_list.append(face_fwd)
        before = shift_prev(conductivity, which)
        face_bwd = shift_prev(face_fwd, which)
        diagonal = diagonal + jnp.where(after > 0, face_fwd, conductivity)
        diagonal = diagonal + jnp.where(before > 0, face_bwd, conductivity)
    divisor = jnp.where(inside, diagonal, 1.0)

    def operate(values_in):
        result = diagonal * values_in
        for which, face_fwd in zip(axes_list, face_list):
            result = result - face_fwd * shift_next(values_in, which)
            result = result - shift_prev(face_fwd * values_in, which)
        return result

    sweep_one = jnp.where(inside, WEIGHT * source / divisor, 0.0)
    sweep_two = jnp.where(inside, sweep_one + WEIGHT * (source - operate(sweep_one)) / divisor, 0.0)
    leftover = jnp.where(inside, source - operate(sweep_two), 0.0)
    return sweep_two, leftover


def restrict(leftover):
    leading = leftover.shape[:-3]
    layers, rows_y, rows_x = leftover.shape[-3:]
    blocks = leftover.reshape(leading + (layers // 2, 2, rows_y // 2, 2, rows_x // 2, 2))
    return jnp.mean(blocks, axis=(-5, -3, -1)).reshape(leading + (-1,))


def reference(source, conductivity, new_owner):
    layers_dev = B_DEV * BZ
    padded = jnp.pad(jnp.stack([source, conductivity]), ((0, 0), (3, 3), (0, 0), (0, 0)))

    def per_device(index):
        start = (index * layers_dev).astype(jnp.int32)
        block = lax.dynamic_slice_in_dim(padded, start, layers_dev + 6, axis=1).astype(jnp.float32)
        sweep_two, leftover = smooth(block[0], block[1])
        settled_box = sweep_two[3:3 + layers_dev].reshape(B_DEV, CELLS).astype(jnp.bfloat16)
        coarse_box = restrict(leftover[3:3 + layers_dev].reshape(B_DEV, BZ, BY, BX))
        return settled_box, coarse_box

    settled, coarse_all = lax.map(per_device, jnp.arange(DEVICES, dtype=jnp.int32))
    coarse = coarse_all.reshape(N_BOX, N_GRP, B_DEV, RC).transpose(1, 0, 2, 3).reshape(N_GRP, N_BOX * B_DEV, RC)
    settled = settled.reshape(N_BOX, N_GRP, B_DEV, CELLS)
    owners = new_owner.reshape(N_BOX, N_GRP, B_DEV)
    order = jnp.arange(B_DEV)
    earlier = (owners[..., :, None] == owners[..., None, :]) & (order[:, None] < order[None, :])
    rank_in = jnp.sum(earlier.astype(jnp.int32), axis=-2).astype(jnp.int32)
    senders = jnp.broadcast_to(jnp.arange(N_BOX, dtype=jnp.int32)[:, None, None], owners.shape)
    groups = jnp.broadcast_to(jnp.arange(N_GRP, dtype=jnp.int32)[None, :, None], owners.shape)
    correction = jnp.zeros((N_BOX, N_GRP, N_GRP, CAP, CELLS), jnp.bfloat16)
    correction = correction.at[senders, owners, groups, rank_in].set(settled)
    return correction, coarse
```

```python
import functools

import jax
import jax.numpy as jnp
from jax import lax
from jax.experimental import pallas as pl
from jax.experimental.pallas import tpu as pltpu
from jax.sharding import PartitionSpec as P

WEIGHT = 0.8
HALO = 3
STEP = 8
MESH = pl.DeviceIdType.MESH


def lane_sub(shape):
    lane = lax.broadcasted_iota(jnp.int32, shape, len(shape) - 1)
    sub = lax.broadcasted_iota(jnp.int32, shape, len(shape) - 2)
    return lane, sub


def y_next(v):
    lane, _ = lane_sub(v.shape)
    a = pltpu.roll(v, 96, 2)
    return jnp.where(lane < 96, a, pltpu.roll(a, 7, 1))


def y_prev(v):
    lane, _ = lane_sub(v.shape)
    a = pltpu.roll(v, 32, 2)
    return jnp.where(lane >= 32, a, pltpu.roll(a, 1, 1))


def x_next(v):
    return pltpu.roll(v, 127, 2)


def x_prev(v):
    return pltpu.roll(v, 1, 2)


def kernel(
    sizes,
    owner_ref,
    source_ref,
    cond_ref,
    corr_ref,
    coarse_ref,
    fc,
    ax_s,
    ay_s,
    az_s,
    inv_s,
    u1_s,
    u2_s,
    t_s,
    boxes,
    slots,
    rs,
    res,
    coarse_s,
    halo_send,
    halo_recv,
    corr_send,
    corr_recv,
    coarse_send,
    coarse_recv,
    local_sem,
):
    n_box, n_grp, nb, layers, ranks = sizes
    total = nb * layers
    me_s, me_g = lax.axis_index("box"), lax.axis_index("grp")
    me = me_s * n_grp + me_g
    count = n_box * n_grp
    after = lax.rem(me + 1, count)
    before = lax.rem(me + count - 1, count)
    after_id = (after // n_grp, lax.rem(after, n_grp))
    before_id = (before // n_grp, lax.rem(before, n_grp))

    barrier = pltpu.get_barrier_semaphore()
    for target in (after_id, before_id):
        pl.semaphore_signal(barrier, inc=1, device_id=target, device_id_type=MESH)

    def greet_grp(off, carry):
        target = (me_s, lax.rem(me_g + off, n_grp))
        pl.semaphore_signal(barrier, inc=1, device_id=target, device_id_type=MESH)
        return carry

    def greet_box(off, carry):
        target = (lax.rem(me_s + off, n_box), me_g)
        pl.semaphore_signal(barrier, inc=1, device_id=target, device_id_type=MESH)
        return carry

    lax.fori_loop(1, n_grp, greet_grp, 0)
    lax.fori_loop(1, n_box, greet_box, 0)

    eye = jnp.where(
        lax.broadcasted_iota(jnp.int32, (total, total), 0)
        == lax.broadcasted_iota(jnp.int32, (total, total), 1),
        1.0,
        0.0,
    ).astype(jnp.bfloat16)
    for which, ref in enumerate((source_ref, cond_ref)):
        for b in range(4):
            turned = lax.dot_general(
                eye,
                ref[pl.ds(b * 256, 256)],
                (((1,), (1,)), ((), ())),
                preferred_element_type=jnp.float32,
            )
            for h in range(2):
                fc[which, pl.ds(HALO * 8 + 2 * b + h, total, stride=8), :] = turned[
                    :, h * 128 : (h + 1) * 128
                ]

    pl.semaphore_wait(barrier, n_grp + n_box)
    to_after = pltpu.make_async_remote_copy(
        src_ref=fc.at[:, pl.ds(total * 8, HALO * 8)],
        dst_ref=fc.at[:, pl.ds(0, HALO * 8)],
        send_sem=halo_send.at[0],
        recv_sem=halo_recv.at[0],
        device_id=after_id,
        device_id_type=MESH,
    )
    to_before = pltpu.make_async_remote_copy(
        src_ref=fc.at[:, pl.ds(HALO * 8, HALO * 8)],
        dst_ref=fc.at[:, pl.ds((total + HALO) * 8, HALO * 8)],
        send_sem=halo_send.at[1],
        recv_sem=halo_recv.at[1],
        device_id=before_id,
        device_id_type=MESH,
    )
    to_after.start()
    to_before.start()

    def field(which, start, n):
        return fc[which, pl.ds(pl.multiple_of(start * 8, 8), n * 8)].reshape(n, 8, 128)

    def first(start, n):
        lane, sub = lane_sub((1, 8, 128))
        x = lane % 32
        y = sub * 4 + lane // 32
        half_x = jnp.where(x != 31, 0.5, 0.0)
        half_y = jnp.where(y != 31, 0.5, 0.0)
        sides = (
            jnp.where(x == 0, 1.0, 0.0)
            + jnp.where(x == 31, 1.0, 0.0)
            + jnp.where(y == 0, 1.0, 0.0)
            + jnp.where(y == 31, 1.0, 0.0)
        )
        slab = field(1, start - 1, n + 2)
        c = slab[1:-1]
        az = 0.5 * (slab[1:] + slab[:-1])
        ax = half_x * (c + x_next(c))
        ay = half_y * (c + y_next(c))
        diag = ax + x_prev(ax) + ay + y_prev(ay) + az[1:] + az[:-1] + sides * c
        inv = WEIGHT / diag
        here = pl.ds(start, n)
        ax_s[here] = ax
        ay_s[here] = ay
        az_s[here] = az[1:]
        inv_s[here] = inv
        u1_s[here] = inv * field(0, start, n)

    def first_step(i, carry):
        first(HALO + i * STEP, STEP)
        return carry

    last = total // STEP - 1
    lax.fori_loop(1, last, first_step, 0, unroll=2)

    def own_slots():
        owners = [owner_ref[k] for k in range(nb)]
        code = []
        for k in range(nb):
            rank = jnp.int32(0)
            for j in range(k):
                rank = rank + jnp.where(owners[j] == owners[k], 1, 0)
            code.append(owners[k] * ranks + rank)
        return code

    code = own_slots()

    to_after.wait_recv()
    to_before.wait_recv()
    to_after.wait_send()
    to_before.wait_send()
    is_first, is_last = me == 0, me == count - 1

    @pl.when(is_first)
    def _():
        outside = pl.ds(0, HALO * 8)
        fc[0, outside] = jnp.zeros((HALO * 8, 128), jnp.float32)
        fc[1, outside] = jnp.concatenate([fc[1, pl.ds(HALO * 8, 8)]] * HALO, axis=0)

    @pl.when(is_last)
    def _():
        outside = pl.ds((total + HALO) * 8, HALO * 8)
        fc[0, outside] = jnp.zeros((HALO * 8, 128), jnp.float32)
        fc[1, outside] = jnp.concatenate([fc[1, pl.ds((total + HALO - 1) * 8, 8)]] * HALO, axis=0)

    first(1, 2 + STEP)
    first(HALO + last * STEP, STEP + 2)

    def near(u, start, n):
        here = pl.ds(start, n)
        ax, ay = ax_s[here], ay_s[here]
        az = az_s[pl.ds(start - 1, n + 1)]
        mid = u[1:-1]
        return (
            ax * x_next(mid)
            + x_prev(ax * mid)
            + ay * y_next(mid)
            + y_prev(ay * mid)
            + az[1:] * u[2:]
            + az[:-1] * u[:-2]
        )

    def second(start, n):
        here = pl.ds(start, n)
        u = u1_s[pl.ds(start - 1, n + 2)]
        nu = near(u, start, n)
        u2 = (2.0 - WEIGHT) * u[1:-1] + inv_s[here] * nu
        u2_s[here] = u2
        return u2, nu

    def second_step(i, carry):
        start = HALO + i * STEP
        u2, nu = second(start, STEP)
        t_s[pl.ds(start, STEP)] = (1.0 - WEIGHT) ** 2 * field(0, start, STEP) - WEIGHT * nu
        per = layers // STEP
        inner = pl.ds(pl.multiple_of(lax.rem(i, per) * STEP * 8, STEP * 8), STEP * 8)
        boxes[i // per, inner] = u2.reshape(STEP * 8, 128).astype(jnp.bfloat16)
        return carry

    lax.fori_loop(0, total // STEP, second_step, 0, unroll=2)
    rows = layers * 8
    boxes[nb] = jnp.zeros((rows, 128), jnp.bfloat16)

    for d in range(n_grp):
        for r in range(ranks):
            pick = jnp.int32(nb)
            for k in range(nb):
                pick = jnp.where(code[k] == d * ranks + r, k, pick)
            slots[d, r] = boxes[pick]

    def corr_copy(off):
        to = lax.rem(me_g + off, n_grp)
        return pltpu.make_async_remote_copy(
            src_ref=slots.at[to],
            dst_ref=corr_ref.at[me_g],
            send_sem=corr_send.at[off],
            recv_sem=corr_recv.at[off],
            device_id=(me_s, to),
            device_id_type=MESH,
        )

    corr_own = pltpu.make_async_copy(slots.at[me_g], corr_ref.at[me_g], local_sem.at[0])

    def corr_start(off, carry):
        corr_copy(off).start()
        return carry

    lax.fori_loop(1, n_grp, corr_start, 0)
    corr_own.start()

    second(HALO - 1, 1)
    second(HALO + total, 1)

    @pl.when(is_first)
    def _():
        u2_s[pl.ds(HALO - 1, 1)] = jnp.zeros((1, 8, 128), jnp.float32)

    @pl.when(is_last)
    def _():
        u2_s[pl.ds(HALO + total, 1)] = jnp.zeros((1, 8, 128), jnp.float32)

    def residual_step(i, carry):
        start = HALO + i * STEP
        u = u2_s[pl.ds(start - 1, STEP + 2)]
        r = t_s[pl.ds(start, STEP)] + near(u, start, STEP)
        for j in range(STEP // 2):
            rs[i * (STEP // 2) + j] = r[2 * j] + r[2 * j + 1]
        return carry

    lax.fori_loop(0, total // STEP, residual_step, 0, unroll=2)

    cell = lax.broadcasted_iota(jnp.int32, (128, 128), 0)
    out = lax.broadcasted_iota(jnp.int32, (128, 128), 1)
    merge = jnp.where(out % 32 == (cell // 64) * 16 + (cell % 32) // 2, 0.125, 0.0).astype(
        jnp.bfloat16
    )
    half = layers // 2

    def restrict_step(k, carry):
        v = rs[pl.ds(k * half, half)].reshape(half * 8, 128)
        high = v.astype(jnp.bfloat16)
        rest = v - high.astype(jnp.float32)
        mid = rest.astype(jnp.bfloat16)
        low = (rest - mid.astype(jnp.float32)).astype(jnp.bfloat16)
        res[...] = (
            jnp.dot(low, merge, preferred_element_type=jnp.float32)
            + jnp.dot(mid, merge, preferred_element_type=jnp.float32)
            + jnp.dot(high, merge, preferred_element_type=jnp.float32)
        )
        lane = lax.broadcasted_iota(jnp.int32, (half * 2, 128), 1) // 32
        value = res[pl.ds(0, half * 2, stride=4), :]
        for p in range(1, 4):
            value = jnp.where(lane == p, res[pl.ds(p, half * 2, stride=4), :], value)
        coarse_s[pl.ds(pl.multiple_of(k * half * 2, half * 2), half * 2)] = value
        return carry

    lax.fori_loop(0, nb, restrict_step, 0)

    crow = nb * half * 2
    mine = pl.ds(pl.multiple_of(me_s * crow, crow), crow)

    def coarse_copy(off):
        return pltpu.make_async_remote_copy(
            src_ref=coarse_s,
            dst_ref=coarse_ref.at[mine],
            send_sem=coarse_send.at[off],
            recv_sem=coarse_recv.at[off],
            device_id=(lax.rem(me_s + off, n_box), me_g),
            device_id_type=MESH,
        )

    def coarse_start(off, carry):
        coarse_copy(off).start()
        return carry

    lax.fori_loop(1, n_box, coarse_start, 0)
    coarse_own = pltpu.make_async_copy(coarse_s, coarse_ref.at[mine], local_sem.at[1])
    coarse_own.start()

    def coarse_wait(off, carry):
        coarse_copy(off).wait()
        return carry

    def corr_wait(off, carry):
        corr_copy(off).wait()
        return carry

    lax.fori_loop(1, n_box, coarse_wait, 0)
    lax.fori_loop(1, n_grp, corr_wait, 0)
    corr_own.wait()
    coarse_own.wait()


def cells_major(field):
    return field.transpose(1, 2, 0).reshape(-1, field.shape[0])


def shards(source, conductivity, new_owner):
    total, rows_y, rows_x = source.shape
    nb = new_owner.shape[2]
    layers = total // nb
    n_box, n_grp = lax.axis_size("box"), lax.axis_size("grp")
    ranks = max(2, (2 * nb + n_grp - 1) // n_grp)
    rows = layers * 8
    deep = total + 2 * HALO
    plane = pltpu.VMEM((deep, 8, 128), jnp.float32)
    crow = total
    corr, coarse = pl.pallas_call(
        functools.partial(kernel, (n_box, n_grp, nb, layers, ranks)),
        out_shape=(
            jax.ShapeDtypeStruct((n_grp, ranks, rows, 128), jnp.bfloat16),
            jax.ShapeDtypeStruct((n_box * crow, 128), jnp.float32),
        ),
        in_specs=[
            pl.BlockSpec(memory_space=pltpu.SMEM),
            pl.BlockSpec(memory_space=pltpu.VMEM),
            pl.BlockSpec(memory_space=pltpu.VMEM),
        ],
        out_specs=[pl.BlockSpec(memory_space=pl.ANY)] * 2,
        scratch_shapes=[
            pltpu.VMEM((2, deep * 8, 128), jnp.float32),
            plane,
            plane,
            plane,
            plane,
            plane,
            plane,
            plane,
            pltpu.VMEM((nb + 1, rows, 128), jnp.bfloat16),
            pltpu.VMEM((n_grp, ranks, rows, 128), jnp.bfloat16),
            pltpu.VMEM((total // 2, 8, 128), jnp.float32),
            pltpu.VMEM((layers // 2 * 8, 128), jnp.float32),
            pltpu.VMEM((crow, 128), jnp.float32),
            pltpu.SemaphoreType.DMA((2,)),
            pltpu.SemaphoreType.DMA((2,)),
            pltpu.SemaphoreType.DMA((n_grp,)),
            pltpu.SemaphoreType.DMA((n_grp,)),
            pltpu.SemaphoreType.DMA((n_box,)),
            pltpu.SemaphoreType.DMA((n_box,)),
            pltpu.SemaphoreType.DMA((2,)),
        ],
        compiler_params=pltpu.CompilerParams(
            collective_id=0, has_side_effects=True, vmem_limit_bytes=40 * 1024 * 1024
        ),
        name="poisson",
    )(new_owner.reshape(nb), cells_major(source), cells_major(conductivity))
    return (
        corr.reshape(1, 1, n_grp, ranks, layers * rows_y * rows_x),
        coarse.reshape(1, n_box * nb, layers * rows_y * rows_x // 8),
    )


def solution(mesh):
    placed = (
        P(("box", "grp"), None, None),
        P(("box", "grp"), None, None),
        P("box", "grp", None, None),
    )
    return jax.shard_map(
        shards,
        mesh=mesh,
        in_specs=placed,
        out_specs=(P("box", "grp", None, None, None), P("grp", None, None)),
        check_vma=False,
    )
```

```python
import functools

import jax
import jax.numpy as jnp
from jax import lax
from jax.experimental import pallas as pl
from jax.experimental.pallas import tpu as pltpu
from jax.sharding import PartitionSpec as P

WEIGHT = 0.8
HALO = 3
EDGE = 2
STEP = 8
MESH = pl.DeviceIdType.MESH


def lane_sub(shape):
    lane = lax.broadcasted_iota(jnp.int32, shape, len(shape) - 1)
    sub = lax.broadcasted_iota(jnp.int32, shape, len(shape) - 2)
    return lane, sub


def y_next(v):
    lane, _ = lane_sub(v.shape)
    a = pltpu.roll(v, 96, 2)
    return jnp.where(lane < 96, a, pltpu.roll(a, 7, 1))


def y_prev(v):
    lane, _ = lane_sub(v.shape)
    a = pltpu.roll(v, 32, 2)
    return jnp.where(lane >= 32, a, pltpu.roll(a, 1, 1))


def x_next(v):
    return pltpu.roll(v, 127, 2)


def x_prev(v):
    return pltpu.roll(v, 1, 2)


def kernel(
    sizes,
    owner_hbm,
    source_hbm,
    cond_hbm,
    corr_ref,
    coarse_ref,
    owner_ref,
    field_s,
    fc,
    ax_s,
    ay_s,
    az_s,
    inv_s,
    u1_s,
    u2_s,
    t_s,
    boxes,
    slots,
    rs,
    res,
    coarse_s,
    halo_send,
    halo_recv,
    corr_send,
    corr_recv,
    coarse_send,
    coarse_recv,
    local_sem,
    input_sem,
):
    n_box, n_grp, nb, layers, ranks = sizes
    total = nb * layers
    me_s, me_g = lax.axis_index("box"), lax.axis_index("grp")
    me = me_s * n_grp + me_g
    count = n_box * n_grp
    after = lax.rem(me + 1, count)
    before = lax.rem(me + count - 1, count)
    after_id = (after // n_grp, lax.rem(after, n_grp))
    before_id = (before // n_grp, lax.rem(before, n_grp))

    quarter = 8 * 32

    def input_copy(which, b):
        part = pl.ds(b * quarter, quarter)
        ref = (source_hbm, cond_hbm)[which]
        return pltpu.make_async_copy(
            ref.at[part], field_s.at[which, part], input_sem.at[which * 4 + b]
        )

    owner_copy = pltpu.make_async_copy(owner_hbm, owner_ref, input_sem.at[8])
    for which in (1, 0):
        for b in range(4):
            input_copy(which, b).start()
    owner_copy.start()

    barrier = pltpu.get_barrier_semaphore()
    for target in (after_id, before_id):
        pl.semaphore_signal(barrier, inc=1, device_id=target, device_id_type=MESH)

    def greet_grp(off, carry):
        target = (me_s, lax.rem(me_g + off, n_grp))
        pl.semaphore_signal(barrier, inc=1, device_id=target, device_id_type=MESH)
        return carry

    def greet_box(off, carry):
        target = (lax.rem(me_s + off, n_box), me_g)
        pl.semaphore_signal(barrier, inc=1, device_id=target, device_id_type=MESH)
        return carry

    lax.fori_loop(1, n_grp, greet_grp, 0)
    lax.fori_loop(1, n_box, greet_box, 0)

    eye = jnp.where(
        lax.broadcasted_iota(jnp.int32, (total, total), 0)
        == lax.broadcasted_iota(jnp.int32, (total, total), 1),
        1.0,
        0.0,
    ).astype(jnp.bfloat16)
    for which in (1, 0):
        for b in range(4):
            input_copy(which, b).wait()
            turned = lax.dot_general(
                eye,
                field_s[which, pl.ds(b * quarter, quarter)],
                (((1,), (1,)), ((), ())),
                preferred_element_type=jnp.float32,
            )
            for h in range(2):
                fc[which, pl.ds(HALO * 8 + 2 * b + h, total, stride=8), :] = turned[
                    :, h * 128 : (h + 1) * 128
                ]

    pl.semaphore_wait(barrier, n_grp + n_box)
    to_after = pltpu.make_async_remote_copy(
        src_ref=fc.at[:, pl.ds(total * 8, HALO * 8)],
        dst_ref=fc.at[:, pl.ds(0, HALO * 8)],
        send_sem=halo_send.at[0],
        recv_sem=halo_recv.at[0],
        device_id=after_id,
        device_id_type=MESH,
    )
    to_before = pltpu.make_async_remote_copy(
        src_ref=fc.at[:, pl.ds(HALO * 8, HALO * 8)],
        dst_ref=fc.at[:, pl.ds((total + HALO) * 8, HALO * 8)],
        send_sem=halo_send.at[1],
        recv_sem=halo_recv.at[1],
        device_id=before_id,
        device_id_type=MESH,
    )
    to_after.start()
    to_before.start()

    def field(which, start, n):
        return fc[which, pl.ds(pl.multiple_of(start * 8, 8), n * 8)].reshape(n, 8, 128)

    def first(start, n):
        lane, sub = lane_sub((1, 8, 128))
        x = lane % 32
        y = sub * 4 + lane // 32
        half_x = jnp.where(x != 31, 0.5, 0.0)
        half_y = jnp.where(y != 31, 0.5, 0.0)
        sides = (
            jnp.where(x == 0, 1.0, 0.0)
            + jnp.where(x == 31, 1.0, 0.0)
            + jnp.where(y == 0, 1.0, 0.0)
            + jnp.where(y == 31, 1.0, 0.0)
        )
        slab = field(1, start - 1, n + 2)
        c = slab[1:-1]
        az = 0.5 * (slab[1:] + slab[:-1])
        ax = half_x * (c + x_next(c))
        ay = half_y * (c + y_next(c))
        diag = ax + x_prev(ax) + ay + y_prev(ay) + az[1:] + az[:-1] + sides * c
        inv = WEIGHT / diag
        here = pl.ds(start, n)
        ax_s[here] = ax
        ay_s[here] = ay
        az_s[here] = az[1:]
        inv_s[here] = inv
        u1_s[here] = inv * field(0, start, n)

    def first_step(i, carry):
        first(HALO + i * STEP, STEP)
        return carry

    last = total // STEP - 1
    tail = HALO + last * STEP
    first(HALO + 1, STEP - 1)
    lax.fori_loop(1, last, first_step, 0, unroll=2)
    first(tail, STEP - 1)

    def near(u, start, n):
        here = pl.ds(start, n)
        ax, ay = ax_s[here], ay_s[here]
        az = az_s[pl.ds(start - 1, n + 1)]
        mid = u[1:-1]
        return (
            ax * x_next(mid)
            + x_prev(ax * mid)
            + ay * y_next(mid)
            + y_prev(ay * mid)
            + az[1:] * u[2:]
            + az[:-1] * u[:-2]
        )

    def second(start, n):
        here = pl.ds(start, n)
        u = u1_s[pl.ds(start - 1, n + 2)]
        nu = near(u, start, n)
        u2 = (2.0 - WEIGHT) * u[1:-1] + inv_s[here] * nu
        u2_s[here] = u2
        return u2, nu

    rows = layers * 8

    def settle(start, n):
        u2, nu = second(start, n)
        t_s[pl.ds(start, n)] = (1.0 - WEIGHT) ** 2 * field(0, start, n) - WEIGHT * nu
        return u2.reshape(n * 8, 128).astype(jnp.bfloat16)

    def second_step(i, carry):
        per = layers // STEP
        inner = pl.ds(pl.multiple_of(lax.rem(i, per) * STEP * 8, STEP * 8), STEP * 8)
        boxes[i // per, inner] = settle(HALO + i * STEP, STEP)
        return carry

    edge = EDGE * 8
    inner_rows = (STEP - EDGE) * 8
    boxes[0, pl.ds(edge, inner_rows)] = settle(HALO + EDGE, STEP - EDGE)
    lax.fori_loop(1, last, second_step, 0, unroll=2)
    boxes[nb - 1, pl.ds(rows - STEP * 8, inner_rows)] = settle(tail, STEP - EDGE)
    boxes[nb] = jnp.zeros((rows, 128), jnp.bfloat16)

    owner_copy.wait()
    def own_slots():
        owners = [owner_ref[k] for k in range(nb)]
        code = []
        for k in range(nb):
            rank = jnp.int32(0)
            for j in range(k):
                rank = rank + jnp.where(owners[j] == owners[k], 1, 0)
            code.append(owners[k] * ranks + rank)
        return code

    code = own_slots()
    picks = []
    for j in range(n_grp * ranks):
        pick = jnp.int32(nb)
        for k in range(nb):
            pick = jnp.where(code[k] == j, k, pick)
        picks.append(pick)

    pieces = (pl.ds(edge, rows - 2 * edge), pl.ds(0, edge), pl.ds(rows - edge, edge))

    def fill(piece):
        for j in range(n_grp * ranks):
            slots[j // ranks, j % ranks, piece] = boxes[picks[j], piece]

    def corr_copy(off, p):
        to = lax.rem(me_g + off, n_grp)
        return pltpu.make_async_remote_copy(
            src_ref=slots.at[to, :, pieces[p]],
            dst_ref=corr_ref.at[me_g, :, pieces[p]],
            send_sem=corr_send.at[off * 3 + p],
            recv_sem=corr_recv.at[off * 3 + p],
            device_id=(me_s, to),
            device_id_type=MESH,
        )

    fill(pieces[0])

    def main_start(off, carry):
        corr_copy(off, 0).start()
        return carry

    lax.fori_loop(1, n_grp, main_start, 0)

    to_after.wait_recv()
    to_before.wait_recv()
    to_after.wait_send()
    to_before.wait_send()
    is_first, is_last = me == 0, me == count - 1

    @pl.when(is_first)
    def _():
        outside = pl.ds(0, HALO * 8)
        fc[0, outside] = jnp.zeros((HALO * 8, 128), jnp.float32)
        fc[1, outside] = jnp.concatenate([fc[1, pl.ds(HALO * 8, 8)]] * HALO, axis=0)

    @pl.when(is_last)
    def _():
        outside = pl.ds((total + HALO) * 8, HALO * 8)
        fc[0, outside] = jnp.zeros((HALO * 8, 128), jnp.float32)
        fc[1, outside] = jnp.concatenate([fc[1, pl.ds((total + HALO - 1) * 8, 8)]] * HALO, axis=0)

    first(1, HALO)
    first(HALO + total - 1, HALO)
    boxes[0, pl.ds(0, edge)] = settle(HALO - 1, EDGE + 1)[8:]
    boxes[nb - 1, pl.ds(rows - edge, edge)] = settle(HALO + total - EDGE, EDGE + 1)[:-8]
    fill(pieces[1])
    fill(pieces[2])

    def edge_start(off, carry):
        corr_copy(off, 1).start()
        corr_copy(off, 2).start()
        return carry

    lax.fori_loop(1, n_grp, edge_start, 0)
    corr_own = pltpu.make_async_copy(slots.at[me_g], corr_ref.at[me_g], local_sem.at[0])
    corr_own.start()

    @pl.when(is_first)
    def _():
        u2_s[pl.ds(HALO - 1, 1)] = jnp.zeros((1, 8, 128), jnp.float32)

    @pl.when(is_last)
    def _():
        u2_s[pl.ds(HALO + total, 1)] = jnp.zeros((1, 8, 128), jnp.float32)

    def residual_step(i, carry):
        start = HALO + i * STEP
        u = u2_s[pl.ds(start - 1, STEP + 2)]
        r = t_s[pl.ds(start, STEP)] + near(u, start, STEP)
        for j in range(STEP // 2):
            rs[i * (STEP // 2) + j] = r[2 * j] + r[2 * j + 1]
        return carry

    lax.fori_loop(0, total // STEP, residual_step, 0, unroll=2)

    cell = lax.broadcasted_iota(jnp.int32, (128, 128), 0)
    out = lax.broadcasted_iota(jnp.int32, (128, 128), 1)
    merge = jnp.where(out % 32 == (cell // 64) * 16 + (cell % 32) // 2, 0.125, 0.0).astype(
        jnp.bfloat16
    )
    half = layers // 2

    def restrict_step(k, carry):
        v = rs[pl.ds(k * half, half)].reshape(half * 8, 128)
        high = v.astype(jnp.bfloat16)
        rest = v - high.astype(jnp.float32)
        mid = rest.astype(jnp.bfloat16)
        low = (rest - mid.astype(jnp.float32)).astype(jnp.bfloat16)
        res[...] = (
            jnp.dot(low, merge, preferred_element_type=jnp.float32)
            + jnp.dot(mid, merge, preferred_element_type=jnp.float32)
            + jnp.dot(high, merge, preferred_element_type=jnp.float32)
        )
        lane = lax.broadcasted_iota(jnp.int32, (half * 2, 128), 1) // 32
        value = res[pl.ds(0, half * 2, stride=4), :]
        for p in range(1, 4):
            value = jnp.where(lane == p, res[pl.ds(p, half * 2, stride=4), :], value)
        coarse_s[pl.ds(pl.multiple_of(k * half * 2, half * 2), half * 2)] = value
        return carry

    lax.fori_loop(0, nb, restrict_step, 0)

    crow = nb * half * 2
    mine = pl.ds(pl.multiple_of(me_s * crow, crow), crow)

    def coarse_copy(off):
        return pltpu.make_async_remote_copy(
            src_ref=coarse_s,
            dst_ref=coarse_ref.at[mine],
            send_sem=coarse_send.at[off],
            recv_sem=coarse_recv.at[off],
            device_id=(lax.rem(me_s + off, n_box), me_g),
            device_id_type=MESH,
        )

    def coarse_start(off, carry):
        coarse_copy(off).start()
        return carry

    lax.fori_loop(1, n_box, coarse_start, 0)
    coarse_own = pltpu.make_async_copy(coarse_s, coarse_ref.at[mine], local_sem.at[1])
    coarse_own.start()

    def coarse_wait(off, carry):
        coarse_copy(off).wait()
        return carry

    def corr_wait(off, carry):
        for p in range(3):
            corr_copy(off, p).wait()
        return carry

    lax.fori_loop(1, n_box, coarse_wait, 0)
    lax.fori_loop(1, n_grp, corr_wait, 0)
    corr_own.wait()
    coarse_own.wait()


def cells_major(field):
    return field.transpose(1, 2, 0).reshape(-1, field.shape[0])


def shards(source, conductivity, new_owner):
    total, rows_y, rows_x = source.shape
    nb = new_owner.shape[2]
    layers = total // nb
    n_box, n_grp = lax.axis_size("box"), lax.axis_size("grp")
    ranks = max(2, (2 * nb + n_grp - 1) // n_grp)
    rows = layers * 8
    deep = total + 2 * HALO
    plane = pltpu.VMEM((deep, 8, 128), jnp.float32)
    crow = total
    corr, coarse = pl.pallas_call(
        functools.partial(kernel, (n_box, n_grp, nb, layers, ranks)),
        out_shape=(
            jax.ShapeDtypeStruct((n_grp, ranks, rows, 128), jnp.bfloat16),
            jax.ShapeDtypeStruct((n_box * crow, 128), jnp.float32),
        ),
        in_specs=[
            pl.BlockSpec(memory_space=pltpu.HBM),
            pl.BlockSpec(memory_space=pltpu.HBM),
            pl.BlockSpec(memory_space=pltpu.HBM),
        ],
        out_specs=[pl.BlockSpec(memory_space=pl.ANY)] * 2,
        scratch_shapes=[
            pltpu.SMEM((nb,), jnp.int32),
            pltpu.VMEM((2, rows_y * rows_x, total), jnp.bfloat16),
            pltpu.VMEM((2, deep * 8, 128), jnp.float32),
            plane,
            plane,
            plane,
            plane,
            plane,
            plane,
            plane,
            pltpu.VMEM((nb + 1, rows, 128), jnp.bfloat16),
            pltpu.VMEM((n_grp, ranks, rows, 128), jnp.bfloat16),
            pltpu.VMEM((total // 2, 8, 128), jnp.float32),
            pltpu.VMEM((layers // 2 * 8, 128), jnp.float32),
            pltpu.VMEM((crow, 128), jnp.float32),
            pltpu.SemaphoreType.DMA((2,)),
            pltpu.SemaphoreType.DMA((2,)),
            pltpu.SemaphoreType.DMA((n_grp * 3,)),
            pltpu.SemaphoreType.DMA((n_grp * 3,)),
            pltpu.SemaphoreType.DMA((n_box,)),
            pltpu.SemaphoreType.DMA((n_box,)),
            pltpu.SemaphoreType.DMA((2,)),
            pltpu.SemaphoreType.DMA((9,)),
        ],
        compiler_params=pltpu.CompilerParams(
            collective_id=0, has_side_effects=True, vmem_limit_bytes=62 * 1024 * 1024
        ),
        name="poisson",
    )(new_owner.reshape(nb), cells_major(source), cells_major(conductivity))
    return (
        corr.reshape(1, 1, n_grp, ranks, layers * rows_y * rows_x),
        coarse.reshape(1, n_box * nb, layers * rows_y * rows_x // 8),
    )


def solution(mesh):
    placed = (
        P(("box", "grp"), None, None),
        P(("box", "grp"), None, None),
        P("box", "grp", None, None),
    )
    return jax.shard_map(
        shards,
        mesh=mesh,
        in_specs=placed,
        out_specs=(P("box", "grp", None, None, None), P("grp", None, None)),
        check_vma=False,
    )
```

```python
import functools

import jax
import jax.numpy as jnp
from jax import lax
from jax.experimental import pallas as pl
from jax.experimental.pallas import tpu as pltpu
from jax.sharding import PartitionSpec as P

WEIGHT = 0.8
HALO = 3
EDGE = 2
STEP = 8
MESH = pl.DeviceIdType.MESH


def lane_sub(shape):
    lane = lax.broadcasted_iota(jnp.int32, shape, len(shape) - 1)
    sub = lax.broadcasted_iota(jnp.int32, shape, len(shape) - 2)
    return lane, sub


def y_next(v):
    lane, _ = lane_sub(v.shape)
    a = pltpu.roll(v, 96, 2)
    return jnp.where(lane < 96, a, pltpu.roll(a, 7, 1))


def y_prev(v):
    lane, _ = lane_sub(v.shape)
    a = pltpu.roll(v, 32, 2)
    return jnp.where(lane >= 32, a, pltpu.roll(a, 1, 1))


def x_next(v):
    return pltpu.roll(v, 127, 2)


def x_prev(v):
    return pltpu.roll(v, 1, 2)


def kernel(
    sizes,
    owner_hbm,
    source_hbm,
    cond_hbm,
    corr_ref,
    coarse_ref,
    owner_ref,
    field_s,
    fc,
    ax_s,
    ay_s,
    az_s,
    inv_s,
    u1_s,
    u2_s,
    t_s,
    boxes,
    slots,
    rs,
    res,
    coarse_s,
    halo_send,
    halo_recv,
    corr_send,
    corr_recv,
    coarse_send,
    coarse_recv,
    local_sem,
    input_sem,
    xs,
    xin,
    xout,
    flags,
    flags_in,
    x_send,
    x_recv,
    f_send,
    flag_send,
    flag_recv,
):
    n_box, n_grp, nb, layers, ranks = sizes
    shared = n_grp == 4 and nb < 2 * ranks
    total = nb * layers
    me_s, me_g = lax.axis_index("box"), lax.axis_index("grp")
    me = me_s * n_grp + me_g
    count = n_box * n_grp
    after = lax.rem(me + 1, count)
    before = lax.rem(me + count - 1, count)
    after_id = (after // n_grp, lax.rem(after, n_grp))
    before_id = (before // n_grp, lax.rem(before, n_grp))

    quarter = 8 * 32

    def input_copy(which, b):
        part = pl.ds(b * quarter, quarter)
        ref = (source_hbm, cond_hbm)[which]
        return pltpu.make_async_copy(
            ref.at[part], field_s.at[which, part], input_sem.at[which * 4 + b]
        )

    owner_copy = pltpu.make_async_copy(owner_hbm, owner_ref, input_sem.at[8])
    for which in (1, 0):
        for b in range(4):
            input_copy(which, b).start()
    owner_copy.start()

    barrier = pltpu.get_barrier_semaphore()
    for target in (after_id, before_id):
        pl.semaphore_signal(barrier, inc=1, device_id=target, device_id_type=MESH)

    def greet_grp(off, carry):
        target = (me_s, lax.rem(me_g + off, n_grp))
        pl.semaphore_signal(barrier, inc=1, device_id=target, device_id_type=MESH)
        return carry

    def greet_box(off, carry):
        target = (lax.rem(me_s + off, n_box), me_g)
        pl.semaphore_signal(barrier, inc=1, device_id=target, device_id_type=MESH)
        return carry

    lax.fori_loop(1, n_grp, greet_grp, 0)
    lax.fori_loop(1, n_box, greet_box, 0)

    eye = jnp.where(
        lax.broadcasted_iota(jnp.int32, (total, total), 0)
        == lax.broadcasted_iota(jnp.int32, (total, total), 1),
        1.0,
        0.0,
    ).astype(jnp.bfloat16)
    for which in (1, 0):
        for b in range(4):
            input_copy(which, b).wait()
            turned = lax.dot_general(
                eye,
                field_s[which, pl.ds(b * quarter, quarter)],
                (((1,), (1,)), ((), ())),
                preferred_element_type=jnp.float32,
            )
            for h in range(2):
                fc[which, pl.ds(HALO * 8 + 2 * b + h, total, stride=8), :] = turned[
                    :, h * 128 : (h + 1) * 128
                ]

    pl.semaphore_wait(barrier, n_grp + n_box)
    to_after = pltpu.make_async_remote_copy(
        src_ref=fc.at[:, pl.ds(total * 8, HALO * 8)],
        dst_ref=fc.at[:, pl.ds(0, HALO * 8)],
        send_sem=halo_send.at[0],
        recv_sem=halo_recv.at[0],
        device_id=after_id,
        device_id_type=MESH,
    )
    to_before = pltpu.make_async_remote_copy(
        src_ref=fc.at[:, pl.ds(HALO * 8, HALO * 8)],
        dst_ref=fc.at[:, pl.ds((total + HALO) * 8, HALO * 8)],
        send_sem=halo_send.at[1],
        recv_sem=halo_recv.at[1],
        device_id=before_id,
        device_id_type=MESH,
    )
    to_after.start()
    to_before.start()

    def field(which, start, n):
        return fc[which, pl.ds(pl.multiple_of(start * 8, 8), n * 8)].reshape(n, 8, 128)

    def first(start, n):
        lane, sub = lane_sub((1, 8, 128))
        x = lane % 32
        y = sub * 4 + lane // 32
        half_x = jnp.where(x != 31, 0.5, 0.0)
        half_y = jnp.where(y != 31, 0.5, 0.0)
        sides = (
            jnp.where(x == 0, 1.0, 0.0)
            + jnp.where(x == 31, 1.0, 0.0)
            + jnp.where(y == 0, 1.0, 0.0)
            + jnp.where(y == 31, 1.0, 0.0)
        )
        slab = field(1, start - 1, n + 2)
        c = slab[1:-1]
        az = 0.5 * (slab[1:] + slab[:-1])
        ax = half_x * (c + x_next(c))
        ay = half_y * (c + y_next(c))
        diag = ax + x_prev(ax) + ay + y_prev(ay) + az[1:] + az[:-1] + sides * c
        inv = WEIGHT / diag
        here = pl.ds(start, n)
        ax_s[here] = ax
        ay_s[here] = ay
        az_s[here] = az[1:]
        inv_s[here] = inv
        u1_s[here] = inv * field(0, start, n)

    def first_step(i, carry):
        first(HALO + i * STEP, STEP)
        return carry

    last = total // STEP - 1
    tail = HALO + last * STEP
    first(HALO + 1, STEP - 1)
    lax.fori_loop(1, last, first_step, 0, unroll=6)
    first(tail, STEP - 1)

    def near(u, start, n):
        here = pl.ds(start, n)
        ax, ay = ax_s[here], ay_s[here]
        az = az_s[pl.ds(start - 1, n + 1)]
        mid = u[1:-1]
        return (
            ax * x_next(mid)
            + x_prev(ax * mid)
            + ay * y_next(mid)
            + y_prev(ay * mid)
            + az[1:] * u[2:]
            + az[:-1] * u[:-2]
        )

    def second(start, n):
        here = pl.ds(start, n)
        u = u1_s[pl.ds(start - 1, n + 2)]
        nu = near(u, start, n)
        u2 = (2.0 - WEIGHT) * u[1:-1] + inv_s[here] * nu
        u2_s[here] = u2
        return u2, nu

    rows = layers * 8

    def settle(start, n):
        u2, nu = second(start, n)
        t_s[pl.ds(start, n)] = (1.0 - WEIGHT) ** 2 * field(0, start, n) - WEIGHT * nu
        return u2.reshape(n * 8, 128).astype(jnp.bfloat16)

    def second_step(i, carry):
        per = layers // STEP
        inner = pl.ds(pl.multiple_of(lax.rem(i, per) * STEP * 8, STEP * 8), STEP * 8)
        boxes[i // per, inner] = settle(HALO + i * STEP, STEP)
        return carry

    edge = EDGE * 8
    inner_rows = (STEP - EDGE) * 8
    boxes[0, pl.ds(edge, inner_rows)] = settle(HALO + EDGE, STEP - EDGE)
    lax.fori_loop(1, last, second_step, 0, unroll=6)
    boxes[nb - 1, pl.ds(rows - STEP * 8, inner_rows)] = settle(tail, STEP - EDGE)
    boxes[nb] = jnp.zeros((rows, 128), jnp.bfloat16)

    owner_copy.wait()
    def own_slots():
        owners = [owner_ref[k] for k in range(nb)]
        code = []
        for k in range(nb):
            rank = jnp.int32(0)
            for j in range(k):
                rank = rank + jnp.where(owners[j] == owners[k], 1, 0)
            code.append(owners[k] * ranks + rank)
        return code

    code = own_slots()
    picks = []
    for j in range(n_grp * ranks):
        pick = jnp.int32(nb)
        for k in range(nb):
            pick = jnp.where(code[k] == j, k, pick)
        picks.append(pick)

    inner, head, foot = (
        pl.ds(edge, rows - 2 * edge),
        pl.ds(0, edge),
        pl.ds(rows - edge, edge),
    )

    half_g = me_g // 2
    partner = me_g + 1 - 2 * lax.rem(me_g, 2)
    near_g, far_g = 2 - half_g, 3 - 3 * half_g
    across = 2 - 2 * half_g
    is_near = me_g == 1 + half_g

    def shared_copy(piece, p):
        return pltpu.make_async_remote_copy(
            src_ref=xs.at[piece],
            dst_ref=xin.at[lax.rem(me_g, 2), piece],
            send_sem=x_send.at[p],
            recv_sem=x_recv.at[lax.rem(me_g, 2) * 3 + p],
            device_id=(me_s, near_g),
            device_id_type=MESH,
        )

    def forward_copy(k, piece, p):
        return pltpu.make_async_remote_copy(
            src_ref=xin.at[k, piece],
            dst_ref=xin.at[k, piece],
            send_sem=f_send.at[k * 3 + p],
            recv_sem=x_recv.at[k * 3 + p],
            device_id=(me_s, partner),
            device_id_type=MESH,
        )

    def flag_copy(to, p):
        return pltpu.make_async_remote_copy(
            src_ref=flags.at[to],
            dst_ref=flags_in.at[me_g],
            send_sem=flag_send.at[p],
            recv_sem=flag_recv.at[me_g],
            device_id=(me_s, to),
            device_id_type=MESH,
        )

    def corr_copy(to, sender, count, p):
        return pltpu.make_async_remote_copy(
            src_ref=slots.at[pl.ds(0, count), to],
            dst_ref=corr_ref.at[pl.ds(0, count), sender],
            send_sem=corr_send.at[p],
            recv_sem=corr_recv.at[sender],
            device_id=(me_s, to),
            device_id_type=MESH,
        )

    if shared:
        lows = [jnp.minimum(picks[2 * h * ranks + ranks - 1], picks[(2 * h + 1) * ranks + ranks - 1]) for h in range(2)]
        pick_x = jnp.where(half_g == 0, lows[1], lows[0])
        xs[inner] = boxes[pick_x, inner]
        shared_copy(inner, 0).start()
        for d in range(n_grp):
            flag = jnp.where(picks[d * ranks + ranks - 1] < nb, 1.0, 0.0)
            flags[d] = jnp.full((16, 128), flag, jnp.float32).astype(jnp.bfloat16)

    to_after.wait_recv()
    to_before.wait_recv()
    to_after.wait_send()
    to_before.wait_send()
    is_first, is_last = me == 0, me == count - 1

    @pl.when(is_first)
    def _():
        outside = pl.ds(0, HALO * 8)
        fc[0, outside] = jnp.zeros((HALO * 8, 128), jnp.float32)
        fc[1, outside] = jnp.concatenate([fc[1, pl.ds(HALO * 8, 8)]] * HALO, axis=0)

    @pl.when(is_last)
    def _():
        outside = pl.ds((total + HALO) * 8, HALO * 8)
        fc[0, outside] = jnp.zeros((HALO * 8, 128), jnp.float32)
        fc[1, outside] = jnp.concatenate([fc[1, pl.ds((total + HALO - 1) * 8, 8)]] * HALO, axis=0)

    first(1, HALO)
    first(HALO + total - 1, HALO)
    boxes[0, pl.ds(0, edge)] = settle(HALO - 1, EDGE + 1)[8:]
    boxes[nb - 1, pl.ds(rows - edge, edge)] = settle(HALO + total - EDGE, EDGE + 1)[:-8]
    if shared:
        xs[head] = boxes[pick_x, head]
        xs[foot] = boxes[pick_x, foot]
        shared_copy(head, 1).start()
        shared_copy(foot, 2).start()
    for j in range(n_grp * ranks):
        slots[j % ranks, j // ranks] = boxes[picks[j]]
    if shared:
        corr_copy(far_g, me_g, ranks - 1, 0).start()
        corr_copy(near_g, me_g, ranks - 1, 1).start()
        corr_copy(partner, me_g, ranks, 2).start()
        flag_copy(near_g, 0).start()
        flag_copy(far_g, 1).start()
    else:

        def corr_start(off, carry):
            corr_copy(lax.rem(me_g + off, n_grp), me_g, ranks, off).start()
            return carry

        lax.fori_loop(1, n_grp, corr_start, 0)
    corr_own = pltpu.make_async_copy(slots.at[:, me_g], corr_ref.at[:, me_g], local_sem.at[0])
    corr_own.start()

    @pl.when(is_first)
    def _():
        u2_s[pl.ds(HALO - 1, 1)] = jnp.zeros((1, 8, 128), jnp.float32)

    @pl.when(is_last)
    def _():
        u2_s[pl.ds(HALO + total, 1)] = jnp.zeros((1, 8, 128), jnp.float32)

    def residual_step(i, carry):
        start = HALO + i * STEP
        u = u2_s[pl.ds(start - 1, STEP + 2)]
        r = t_s[pl.ds(start, STEP)] + near(u, start, STEP)
        for j in range(STEP // 2):
            rs[i * (STEP // 2) + j] = r[2 * j] + r[2 * j + 1]
        return carry

    lax.fori_loop(0, total // STEP, residual_step, 0, unroll=5)

    cell = lax.broadcasted_iota(jnp.int32, (128, 128), 0)
    out = lax.broadcasted_iota(jnp.int32, (128, 128), 1)
    merge = jnp.where(out % 32 == (cell // 64) * 16 + (cell % 32) // 2, 0.125, 0.0).astype(
        jnp.bfloat16
    )
    half = layers // 2

    def restrict_step(k, carry):
        v = rs[pl.ds(k * half, half)].reshape(half * 8, 128)
        high = v.astype(jnp.bfloat16)
        rest = v - high.astype(jnp.float32)
        mid = rest.astype(jnp.bfloat16)
        low = (rest - mid.astype(jnp.float32)).astype(jnp.bfloat16)
        res[...] = (
            jnp.dot(low, merge, preferred_element_type=jnp.float32)
            + jnp.dot(mid, merge, preferred_element_type=jnp.float32)
            + jnp.dot(high, merge, preferred_element_type=jnp.float32)
        )
        lane = lax.broadcasted_iota(jnp.int32, (half * 2, 128), 1) // 32
        value = res[pl.ds(0, half * 2, stride=4), :]
        for p in range(1, 4):
            value = jnp.where(lane == p, res[pl.ds(p, half * 2, stride=4), :], value)
        coarse_s[pl.ds(pl.multiple_of(k * half * 2, half * 2), half * 2)] = value
        return carry

    lax.fori_loop(0, nb, restrict_step, 0)

    crow = nb * half * 2
    mine = pl.ds(pl.multiple_of(me_s * crow, crow), crow)

    def coarse_copy(off):
        return pltpu.make_async_remote_copy(
            src_ref=coarse_s,
            dst_ref=coarse_ref.at[mine],
            send_sem=coarse_send.at[off],
            recv_sem=coarse_recv.at[off],
            device_id=(lax.rem(me_s + off, n_box), me_g),
            device_id_type=MESH,
        )

    def coarse_start(off, carry):
        coarse_copy(off).start()
        return carry

    lax.fori_loop(1, n_box, coarse_start, 0)
    coarse_own = pltpu.make_async_copy(coarse_s, coarse_ref.at[mine], local_sem.at[1])
    coarse_own.start()

    def coarse_wait(off, carry):
        coarse_copy(off).wait()
        return carry

    if shared:
        whole = (inner, head, foot)
        for k in range(2):
            for p in range(3):
                forward_copy(k, whole[p], p).wait_recv()

            @pl.when(is_near)
            def _():
                for p in range(3):
                    forward_copy(k, whole[p], p).start()

        for k in range(2):
            flag_copy_in = pltpu.make_async_remote_copy(
                src_ref=flags.at[0],
                dst_ref=flags_in.at[across + k],
                send_sem=flag_send.at[0],
                recv_sem=flag_recv.at[across + k],
                device_id=(me_s, partner),
                device_id_type=MESH,
            )
            flag_copy_in.wait_recv()
            kept = xin[k].reshape(rows // 16, 16, 128) * flags_in[across + k][None]
            xout[k] = kept.reshape(rows, 128)
            pltpu.make_async_copy(
                xout.at[k], corr_ref.at[ranks - 1, across + k], local_sem.at[2 + k]
            ).start()

    lax.fori_loop(1, n_box, coarse_wait, 0)
    if shared:
        for k in range(2):
            pltpu.make_async_copy(
                xout.at[k], corr_ref.at[ranks - 1, across + k], local_sem.at[2 + k]
            ).wait()
            corr_copy(partner, across + k, ranks - 1, 0).wait_recv()
        corr_copy(partner, partner, ranks, 2).wait_recv()
        corr_copy(far_g, me_g, ranks - 1, 0).wait_send()
        corr_copy(near_g, me_g, ranks - 1, 1).wait_send()
        corr_copy(partner, me_g, ranks, 2).wait_send()
        flag_copy(near_g, 0).wait_send()
        flag_copy(far_g, 1).wait_send()
        for p in range(3):
            shared_copy(whole[p], p).wait_send()

        @pl.when(is_near)
        def _():
            for k in range(2):
                for p in range(3):
                    forward_copy(k, whole[p], p).wait_send()

    else:

        def corr_wait(off, carry):
            corr_copy(lax.rem(me_g + off, n_grp), me_g, ranks, off).wait_send()
            sender = lax.rem(me_g + off, n_grp)
            corr_copy(sender, sender, ranks, off).wait_recv()
            return carry

        lax.fori_loop(1, n_grp, corr_wait, 0)
    corr_own.wait()
    coarse_own.wait()


def cells_major(field):
    return field.transpose(1, 2, 0).reshape(-1, field.shape[0])


def shards(source, conductivity, new_owner):
    total, rows_y, rows_x = source.shape
    nb = new_owner.shape[2]
    layers = total // nb
    n_box, n_grp = lax.axis_size("box"), lax.axis_size("grp")
    ranks = max(2, (2 * nb + n_grp - 1) // n_grp)
    rows = layers * 8
    deep = total + 2 * HALO
    plane = pltpu.VMEM((deep, 8, 128), jnp.float32)
    crow = total
    corr, coarse = pl.pallas_call(
        functools.partial(kernel, (n_box, n_grp, nb, layers, ranks)),
        out_shape=(
            jax.ShapeDtypeStruct((ranks, n_grp, rows, 128), jnp.bfloat16),
            jax.ShapeDtypeStruct((n_box * crow, 128), jnp.float32),
        ),
        in_specs=[
            pl.BlockSpec(memory_space=pltpu.HBM),
            pl.BlockSpec(memory_space=pltpu.HBM),
            pl.BlockSpec(memory_space=pltpu.HBM),
        ],
        out_specs=[pl.BlockSpec(memory_space=pl.ANY)] * 2,
        scratch_shapes=[
            pltpu.SMEM((nb,), jnp.int32),
            pltpu.VMEM((2, rows_y * rows_x, total), jnp.bfloat16),
            pltpu.VMEM((2, deep * 8, 128), jnp.float32),
            plane,
            plane,
            plane,
            plane,
            plane,
            plane,
            plane,
            pltpu.VMEM((nb + 1, rows, 128), jnp.bfloat16),
            pltpu.VMEM((ranks, n_grp, rows, 128), jnp.bfloat16),
            pltpu.VMEM((total // 2, 8, 128), jnp.float32),
            pltpu.VMEM((layers // 2 * 8, 128), jnp.float32),
            pltpu.VMEM((crow, 128), jnp.float32),
            pltpu.SemaphoreType.DMA((2,)),
            pltpu.SemaphoreType.DMA((2,)),
            pltpu.SemaphoreType.DMA((n_grp,)),
            pltpu.SemaphoreType.DMA((n_grp,)),
            pltpu.SemaphoreType.DMA((n_box,)),
            pltpu.SemaphoreType.DMA((n_box,)),
            pltpu.SemaphoreType.DMA((4,)),
            pltpu.SemaphoreType.DMA((9,)),
            pltpu.VMEM((rows, 128), jnp.bfloat16),
            pltpu.VMEM((2, rows, 128), jnp.bfloat16),
            pltpu.VMEM((2, rows, 128), jnp.bfloat16),
            pltpu.VMEM((n_grp, 16, 128), jnp.bfloat16),
            pltpu.VMEM((n_grp, 16, 128), jnp.bfloat16),
            pltpu.SemaphoreType.DMA((3,)),
            pltpu.SemaphoreType.DMA((6,)),
            pltpu.SemaphoreType.DMA((6,)),
            pltpu.SemaphoreType.DMA((2,)),
            pltpu.SemaphoreType.DMA((n_grp,)),
        ],
        compiler_params=pltpu.CompilerParams(
            collective_id=0, has_side_effects=True, vmem_limit_bytes=62 * 1024 * 1024
        ),
        name="poisson",
    )(new_owner.reshape(nb), cells_major(source), cells_major(conductivity))
    return (
        corr.reshape(ranks, n_grp, rows * 128).transpose(1, 0, 2)[None, None],
        coarse.reshape(1, n_box * nb, layers * rows_y * rows_x // 8),
    )


def solution(mesh):
    placed = (
        P(("box", "grp"), None, None),
        P(("box", "grp"), None, None),
        P("box", "grp", None, None),
    )
    return jax.shard_map(
        shards,
        mesh=mesh,
        in_specs=placed,
        out_specs=(P("box", "grp", None, None, None), P("grp", None, None)),
        check_vma=False,
    )
```

```python
import functools

import jax
import jax.numpy as jnp
from jax import lax
from jax.experimental import pallas as pl
from jax.experimental.pallas import tpu as pltpu
from jax.sharding import PartitionSpec as P

WEIGHT = 0.8
HALO = 3
EDGE = 2
STEP = 8
MESH = pl.DeviceIdType.MESH


def lane_sub(shape):
    lane = lax.broadcasted_iota(jnp.int32, shape, len(shape) - 1)
    sub = lax.broadcasted_iota(jnp.int32, shape, len(shape) - 2)
    return lane, sub


def y_next(v):
    lane, _ = lane_sub(v.shape)
    a = pltpu.roll(v, 96, 2)
    return jnp.where(lane < 96, a, pltpu.roll(a, 7, 1))


def y_prev(v):
    lane, _ = lane_sub(v.shape)
    a = pltpu.roll(v, 32, 2)
    return jnp.where(lane >= 32, a, pltpu.roll(a, 1, 1))


def x_next(v):
    return pltpu.roll(v, 127, 2)


def x_prev(v):
    return pltpu.roll(v, 1, 2)


def kernel(
    sizes,
    owner_hbm,
    source_hbm,
    cond_hbm,
    corr_ref,
    coarse_ref,
    owner_ref,
    field_s,
    fc,
    ax_s,
    ay_s,
    az_s,
    inv_s,
    u1_s,
    u2_s,
    t_s,
    boxes,
    slots,
    rs,
    res,
    coarse_s,
    halo_send,
    halo_recv,
    corr_send,
    corr_recv,
    coarse_send,
    coarse_recv,
    local_sem,
    input_sem,
    xs,
    xin,
    xout,
    flags,
    flags_in,
    x_send,
    x_recv,
    f_send,
    flag_send,
    flag_recv,
    far_send,
    far_recv,
):
    n_box, n_grp, nb, layers, ranks = sizes
    shared = n_grp == 4 and nb < 2 * ranks
    total = nb * layers
    me_s, me_g = lax.axis_index("box"), lax.axis_index("grp")
    me = me_s * n_grp + me_g
    count = n_box * n_grp
    after = lax.rem(me + 1, count)
    before = lax.rem(me + count - 1, count)
    after_id = (after // n_grp, lax.rem(after, n_grp))
    before_id = (before // n_grp, lax.rem(before, n_grp))

    quarter = 8 * 32

    def input_copy(which, b):
        part = pl.ds(b * quarter, quarter)
        ref = (source_hbm, cond_hbm)[which]
        return pltpu.make_async_copy(
            ref.at[part], field_s.at[which, part], input_sem.at[which * 4 + b]
        )

    owner_copy = pltpu.make_async_copy(owner_hbm, owner_ref, input_sem.at[8])
    for which in (1, 0):
        for b in range(4):
            input_copy(which, b).start()
    owner_copy.start()

    barrier = pltpu.get_barrier_semaphore()
    for target in (after_id, before_id):
        pl.semaphore_signal(barrier, inc=1, device_id=target, device_id_type=MESH)

    def greet_grp(off, carry):
        target = (me_s, lax.rem(me_g + off, n_grp))
        pl.semaphore_signal(barrier, inc=1, device_id=target, device_id_type=MESH)
        return carry

    def greet_box(off, carry):
        target = (lax.rem(me_s + off, n_box), me_g)
        pl.semaphore_signal(barrier, inc=1, device_id=target, device_id_type=MESH)
        return carry

    lax.fori_loop(1, n_grp, greet_grp, 0)
    lax.fori_loop(1, n_box, greet_box, 0)

    eye = jnp.where(
        lax.broadcasted_iota(jnp.int32, (total, total), 0)
        == lax.broadcasted_iota(jnp.int32, (total, total), 1),
        1.0,
        0.0,
    ).astype(jnp.bfloat16)
    for which in (1, 0):
        for b in range(4):
            input_copy(which, b).wait()
            turned = lax.dot_general(
                eye,
                field_s[which, pl.ds(b * quarter, quarter)],
                (((1,), (1,)), ((), ())),
                preferred_element_type=jnp.float32,
            )
            for h in range(2):
                fc[which, pl.ds(HALO * 8 + 2 * b + h, total, stride=8), :] = turned[
                    :, h * 128 : (h + 1) * 128
                ]

    pl.semaphore_wait(barrier, n_grp + n_box)
    to_after = pltpu.make_async_remote_copy(
        src_ref=fc.at[:, pl.ds(total * 8, HALO * 8)],
        dst_ref=fc.at[:, pl.ds(0, HALO * 8)],
        send_sem=halo_send.at[0],
        recv_sem=halo_recv.at[0],
        device_id=after_id,
        device_id_type=MESH,
    )
    to_before = pltpu.make_async_remote_copy(
        src_ref=fc.at[:, pl.ds(HALO * 8, HALO * 8)],
        dst_ref=fc.at[:, pl.ds((total + HALO) * 8, HALO * 8)],
        send_sem=halo_send.at[1],
        recv_sem=halo_recv.at[1],
        device_id=before_id,
        device_id_type=MESH,
    )
    to_after.start()
    to_before.start()

    def field(which, start, n):
        return fc[which, pl.ds(pl.multiple_of(start * 8, 8), n * 8)].reshape(n, 8, 128)

    def first(start, n):
        lane, sub = lane_sub((1, 8, 128))
        x = lane % 32
        y = sub * 4 + lane // 32
        half_x = jnp.where(x != 31, 0.5, 0.0)
        half_y = jnp.where(y != 31, 0.5, 0.0)
        sides = (
            jnp.where(x == 0, 1.0, 0.0)
            + jnp.where(x == 31, 1.0, 0.0)
            + jnp.where(y == 0, 1.0, 0.0)
            + jnp.where(y == 31, 1.0, 0.0)
        )
        slab = field(1, start - 1, n + 2)
        c = slab[1:-1]
        az = 0.5 * (slab[1:] + slab[:-1])
        ax = half_x * (c + x_next(c))
        ay = half_y * (c + y_next(c))
        diag = ax + x_prev(ax) + ay + y_prev(ay) + az[1:] + az[:-1] + sides * c
        inv = WEIGHT / diag
        here = pl.ds(start, n)
        ax_s[here] = ax
        ay_s[here] = ay
        az_s[here] = az[1:]
        inv_s[here] = inv
        u1_s[here] = inv * field(0, start, n)

    def first_step(i, carry):
        first(HALO + i * STEP, STEP)
        return carry

    last = total // STEP - 1
    tail = HALO + last * STEP
    first(HALO + 1, STEP - 1)
    lax.fori_loop(1, last, first_step, 0, unroll=6)
    first(tail, STEP - 1)

    def near(u, start, n):
        here = pl.ds(start, n)
        ax, ay = ax_s[here], ay_s[here]
        az = az_s[pl.ds(start - 1, n + 1)]
        mid = u[1:-1]
        return (
            ax * x_next(mid)
            + x_prev(ax * mid)
            + ay * y_next(mid)
            + y_prev(ay * mid)
            + az[1:] * u[2:]
            + az[:-1] * u[:-2]
        )

    def second(start, n):
        here = pl.ds(start, n)
        u = u1_s[pl.ds(start - 1, n + 2)]
        nu = near(u, start, n)
        u2 = (2.0 - WEIGHT) * u[1:-1] + inv_s[here] * nu
        u2_s[here] = u2
        return u2, nu

    rows = layers * 8

    def settle(start, n):
        u2, nu = second(start, n)
        t_s[pl.ds(start, n)] = (1.0 - WEIGHT) ** 2 * field(0, start, n) - WEIGHT * nu
        return u2.reshape(n * 8, 128).astype(jnp.bfloat16)

    def second_step(i, carry):
        per = layers // STEP
        inner = pl.ds(pl.multiple_of(lax.rem(i, per) * STEP * 8, STEP * 8), STEP * 8)
        boxes[i // per, inner] = settle(HALO + i * STEP, STEP)
        return carry

    edge = EDGE * 8
    inner_rows = (STEP - EDGE) * 8
    boxes[0, pl.ds(edge, inner_rows)] = settle(HALO + EDGE, STEP - EDGE)
    lax.fori_loop(1, last, second_step, 0, unroll=6)
    boxes[nb - 1, pl.ds(rows - STEP * 8, inner_rows)] = settle(tail, STEP - EDGE)
    boxes[nb] = jnp.zeros((rows, 128), jnp.bfloat16)

    owner_copy.wait()
    def own_slots():
        owners = [owner_ref[k] for k in range(nb)]
        code = []
        for k in range(nb):
            rank = jnp.int32(0)
            for j in range(k):
                rank = rank + jnp.where(owners[j] == owners[k], 1, 0)
            code.append(owners[k] * ranks + rank)
        return code

    code = own_slots()
    picks = []
    for j in range(n_grp * ranks):
        pick = jnp.int32(nb)
        for k in range(nb):
            pick = jnp.where(code[k] == j, k, pick)
        picks.append(pick)

    inner, head, foot = (
        pl.ds(edge, rows - 2 * edge),
        pl.ds(0, edge),
        pl.ds(rows - edge, edge),
    )

    half_g = me_g // 2
    partner = me_g + 1 - 2 * lax.rem(me_g, 2)
    near_g, far_g = 2 - half_g, 3 - 3 * half_g
    across = 2 - 2 * half_g
    is_near = me_g == 1 + half_g

    def shared_copy(piece, p):
        return pltpu.make_async_remote_copy(
            src_ref=xs.at[piece],
            dst_ref=xin.at[lax.rem(me_g, 2), piece],
            send_sem=x_send.at[p],
            recv_sem=x_recv.at[lax.rem(me_g, 2) * 3 + p],
            device_id=(me_s, near_g),
            device_id_type=MESH,
        )

    def forward_copy(k, piece, p):
        return pltpu.make_async_remote_copy(
            src_ref=xin.at[k, piece],
            dst_ref=xin.at[k, piece],
            send_sem=f_send.at[k * 3 + p],
            recv_sem=x_recv.at[k * 3 + p],
            device_id=(me_s, partner),
            device_id_type=MESH,
        )

    def flag_copy(to, p):
        return pltpu.make_async_remote_copy(
            src_ref=flags.at[to],
            dst_ref=flags_in.at[me_g],
            send_sem=flag_send.at[p],
            recv_sem=flag_recv.at[me_g],
            device_id=(me_s, to),
            device_id_type=MESH,
        )

    whole = (inner, head, foot)

    def far_copy(to, sender, p):
        return pltpu.make_async_remote_copy(
            src_ref=slots.at[pl.ds(0, ranks - 1), to, whole[p]],
            dst_ref=corr_ref.at[pl.ds(0, ranks - 1), sender, whole[p]],
            send_sem=far_send.at[p],
            recv_sem=far_recv.at[lax.rem(sender, 2) * 3 + p],
            device_id=(me_s, to),
            device_id_type=MESH,
        )

    def fill(part):
        for j in range(n_grp * ranks):
            slots[j % ranks, j // ranks, part] = boxes[picks[j], part]

    def corr_copy(to, sender, count, p):
        return pltpu.make_async_remote_copy(
            src_ref=slots.at[pl.ds(0, count), to],
            dst_ref=corr_ref.at[pl.ds(0, count), sender],
            send_sem=corr_send.at[p],
            recv_sem=corr_recv.at[sender],
            device_id=(me_s, to),
            device_id_type=MESH,
        )

    if shared:
        lows = [jnp.minimum(picks[2 * h * ranks + ranks - 1], picks[(2 * h + 1) * ranks + ranks - 1]) for h in range(2)]
        pick_x = jnp.where(half_g == 0, lows[1], lows[0])
        xs[inner] = boxes[pick_x, inner]
        shared_copy(inner, 0).start()
    fill(inner)
    if shared:
        far_copy(far_g, me_g, 0).start()
        for d in range(n_grp):
            flag = jnp.where(picks[d * ranks + ranks - 1] < nb, 1.0, 0.0)
            flags[d] = jnp.full((16, 128), flag, jnp.float32).astype(jnp.bfloat16)

    to_after.wait_recv()
    to_before.wait_recv()
    to_after.wait_send()
    to_before.wait_send()
    is_first, is_last = me == 0, me == count - 1

    @pl.when(is_first)
    def _():
        outside = pl.ds(0, HALO * 8)
        fc[0, outside] = jnp.zeros((HALO * 8, 128), jnp.float32)
        fc[1, outside] = jnp.concatenate([fc[1, pl.ds(HALO * 8, 8)]] * HALO, axis=0)

    @pl.when(is_last)
    def _():
        outside = pl.ds((total + HALO) * 8, HALO * 8)
        fc[0, outside] = jnp.zeros((HALO * 8, 128), jnp.float32)
        fc[1, outside] = jnp.concatenate([fc[1, pl.ds((total + HALO - 1) * 8, 8)]] * HALO, axis=0)

    first(1, HALO)
    first(HALO + total - 1, HALO)
    boxes[0, pl.ds(0, edge)] = settle(HALO - 1, EDGE + 1)[8:]
    boxes[nb - 1, pl.ds(rows - edge, edge)] = settle(HALO + total - EDGE, EDGE + 1)[:-8]
    if shared:
        xs[head] = boxes[pick_x, head]
        xs[foot] = boxes[pick_x, foot]
        shared_copy(head, 1).start()
        shared_copy(foot, 2).start()
    fill(head)
    fill(foot)
    if shared:
        far_copy(far_g, me_g, 1).start()
        far_copy(far_g, me_g, 2).start()
        corr_copy(near_g, me_g, ranks - 1, 1).start()
        corr_copy(partner, me_g, ranks, 2).start()
        flag_copy(near_g, 0).start()
        flag_copy(far_g, 1).start()
    else:

        def corr_start(off, carry):
            corr_copy(lax.rem(me_g + off, n_grp), me_g, ranks, off).start()
            return carry

        lax.fori_loop(1, n_grp, corr_start, 0)
    corr_own = pltpu.make_async_copy(slots.at[:, me_g], corr_ref.at[:, me_g], local_sem.at[0])
    corr_own.start()

    @pl.when(is_first)
    def _():
        u2_s[pl.ds(HALO - 1, 1)] = jnp.zeros((1, 8, 128), jnp.float32)

    @pl.when(is_last)
    def _():
        u2_s[pl.ds(HALO + total, 1)] = jnp.zeros((1, 8, 128), jnp.float32)

    def residual_step(i, carry):
        start = HALO + i * STEP
        u = u2_s[pl.ds(start - 1, STEP + 2)]
        r = t_s[pl.ds(start, STEP)] + near(u, start, STEP)
        for j in range(STEP // 2):
            rs[i * (STEP // 2) + j] = r[2 * j] + r[2 * j + 1]
        return carry

    lax.fori_loop(0, total // STEP, residual_step, 0, unroll=5)

    cell = lax.broadcasted_iota(jnp.int32, (128, 128), 0)
    out = lax.broadcasted_iota(jnp.int32, (128, 128), 1)
    merge = jnp.where(out % 32 == (cell // 64) * 16 + (cell % 32) // 2, 0.125, 0.0).astype(
        jnp.bfloat16
    )
    half = layers // 2

    def restrict_step(k, carry):
        v = rs[pl.ds(k * half, half)].reshape(half * 8, 128)
        high = v.astype(jnp.bfloat16)
        rest = v - high.astype(jnp.float32)
        mid = rest.astype(jnp.bfloat16)
        low = (rest - mid.astype(jnp.float32)).astype(jnp.bfloat16)
        res[...] = (
            jnp.dot(low, merge, preferred_element_type=jnp.float32)
            + jnp.dot(mid, merge, preferred_element_type=jnp.float32)
            + jnp.dot(high, merge, preferred_element_type=jnp.float32)
        )
        lane = lax.broadcasted_iota(jnp.int32, (half * 2, 128), 1) // 32
        value = res[pl.ds(0, half * 2, stride=4), :]
        for p in range(1, 4):
            value = jnp.where(lane == p, res[pl.ds(p, half * 2, stride=4), :], value)
        coarse_s[pl.ds(pl.multiple_of(k * half * 2, half * 2), half * 2)] = value
        return carry

    lax.fori_loop(0, nb, restrict_step, 0)

    crow = nb * half * 2
    mine = pl.ds(pl.multiple_of(me_s * crow, crow), crow)

    def coarse_copy(off):
        return pltpu.make_async_remote_copy(
            src_ref=coarse_s,
            dst_ref=coarse_ref.at[mine],
            send_sem=coarse_send.at[off],
            recv_sem=coarse_recv.at[off],
            device_id=(lax.rem(me_s + off, n_box), me_g),
            device_id_type=MESH,
        )

    def coarse_start(off, carry):
        coarse_copy(off).start()
        return carry

    lax.fori_loop(1, n_box, coarse_start, 0)
    coarse_own = pltpu.make_async_copy(coarse_s, coarse_ref.at[mine], local_sem.at[1])
    coarse_own.start()

    def coarse_wait(off, carry):
        coarse_copy(off).wait()
        return carry

    if shared:
        for p in range(3):
            for k in range(2):
                forward_copy(k, whole[p], p).wait_recv()

                @pl.when(is_near)
                def _():
                    forward_copy(k, whole[p], p).start()

        for k in range(2):
            flag_copy_in = pltpu.make_async_remote_copy(
                src_ref=flags.at[0],
                dst_ref=flags_in.at[across + k],
                send_sem=flag_send.at[0],
                recv_sem=flag_recv.at[across + k],
                device_id=(me_s, partner),
                device_id_type=MESH,
            )
            flag_copy_in.wait_recv()
            kept = xin[k].reshape(rows // 16, 16, 128) * flags_in[across + k][None]
            xout[k] = kept.reshape(rows, 128)
            pltpu.make_async_copy(
                xout.at[k], corr_ref.at[ranks - 1, across + k], local_sem.at[2 + k]
            ).start()

    lax.fori_loop(1, n_box, coarse_wait, 0)
    if shared:
        for k in range(2):
            pltpu.make_async_copy(
                xout.at[k], corr_ref.at[ranks - 1, across + k], local_sem.at[2 + k]
            ).wait()

            @pl.when(is_near)
            def _():
                corr_copy(partner, across + k, ranks - 1, 0).wait_recv()

            @pl.when(jnp.logical_not(is_near))
            def _():
                for p in range(3):
                    far_copy(partner, across + k, p).wait_recv()

        corr_copy(partner, partner, ranks, 2).wait_recv()
        for p in range(3):
            far_copy(far_g, me_g, p).wait_send()
        corr_copy(near_g, me_g, ranks - 1, 1).wait_send()
        corr_copy(partner, me_g, ranks, 2).wait_send()
        flag_copy(near_g, 0).wait_send()
        flag_copy(far_g, 1).wait_send()
        for p in range(3):
            shared_copy(whole[p], p).wait_send()

        @pl.when(is_near)
        def _():
            for k in range(2):
                for p in range(3):
                    forward_copy(k, whole[p], p).wait_send()

    else:

        def corr_wait(off, carry):
            corr_copy(lax.rem(me_g + off, n_grp), me_g, ranks, off).wait_send()
            sender = lax.rem(me_g + off, n_grp)
            corr_copy(sender, sender, ranks, off).wait_recv()
            return carry

        lax.fori_loop(1, n_grp, corr_wait, 0)
    corr_own.wait()
    coarse_own.wait()


def cells_major(field):
    return field.transpose(1, 2, 0).reshape(-1, field.shape[0])


def shards(source, conductivity, new_owner):
    total, rows_y, rows_x = source.shape
    nb = new_owner.shape[2]
    layers = total // nb
    n_box, n_grp = lax.axis_size("box"), lax.axis_size("grp")
    ranks = max(2, (2 * nb + n_grp - 1) // n_grp)
    rows = layers * 8
    deep = total + 2 * HALO
    plane = pltpu.VMEM((deep, 8, 128), jnp.float32)
    crow = total
    corr, coarse = pl.pallas_call(
        functools.partial(kernel, (n_box, n_grp, nb, layers, ranks)),
        out_shape=(
            jax.ShapeDtypeStruct((ranks, n_grp, rows, 128), jnp.bfloat16),
            jax.ShapeDtypeStruct((n_box * crow, 128), jnp.float32),
        ),
        in_specs=[
            pl.BlockSpec(memory_space=pltpu.HBM),
            pl.BlockSpec(memory_space=pltpu.HBM),
            pl.BlockSpec(memory_space=pltpu.HBM),
        ],
        out_specs=[pl.BlockSpec(memory_space=pl.ANY)] * 2,
        scratch_shapes=[
            pltpu.SMEM((nb,), jnp.int32),
            pltpu.VMEM((2, rows_y * rows_x, total), jnp.bfloat16),
            pltpu.VMEM((2, deep * 8, 128), jnp.float32),
            plane,
            plane,
            plane,
            plane,
            plane,
            plane,
            plane,
            pltpu.VMEM((nb + 1, rows, 128), jnp.bfloat16),
            pltpu.VMEM((ranks, n_grp, rows, 128), jnp.bfloat16),
            pltpu.VMEM((total // 2, 8, 128), jnp.float32),
            pltpu.VMEM((layers // 2 * 8, 128), jnp.float32),
            pltpu.VMEM((crow, 128), jnp.float32),
            pltpu.SemaphoreType.DMA((2,)),
            pltpu.SemaphoreType.DMA((2,)),
            pltpu.SemaphoreType.DMA((n_grp,)),
            pltpu.SemaphoreType.DMA((n_grp,)),
            pltpu.SemaphoreType.DMA((n_box,)),
            pltpu.SemaphoreType.DMA((n_box,)),
            pltpu.SemaphoreType.DMA((4,)),
            pltpu.SemaphoreType.DMA((9,)),
            pltpu.VMEM((rows, 128), jnp.bfloat16),
            pltpu.VMEM((2, rows, 128), jnp.bfloat16),
            pltpu.VMEM((2, rows, 128), jnp.bfloat16),
            pltpu.VMEM((n_grp, 16, 128), jnp.bfloat16),
            pltpu.VMEM((n_grp, 16, 128), jnp.bfloat16),
            pltpu.SemaphoreType.DMA((3,)),
            pltpu.SemaphoreType.DMA((6,)),
            pltpu.SemaphoreType.DMA((6,)),
            pltpu.SemaphoreType.DMA((2,)),
            pltpu.SemaphoreType.DMA((n_grp,)),
            pltpu.SemaphoreType.DMA((3,)),
            pltpu.SemaphoreType.DMA((6,)),
        ],
        compiler_params=pltpu.CompilerParams(
            collective_id=0, has_side_effects=True, vmem_limit_bytes=62 * 1024 * 1024
        ),
        name="poisson",
    )(new_owner.reshape(nb), cells_major(source), cells_major(conductivity))
    return (
        corr.reshape(ranks, n_grp, rows * 128).transpose(1, 0, 2)[None, None],
        coarse.reshape(1, n_box * nb, layers * rows_y * rows_x // 8),
    )


def solution(mesh):
    placed = (
        P(("box", "grp"), None, None),
        P(("box", "grp"), None, None),
        P("box", "grp", None, None),
    )
    return jax.shard_map(
        shards,
        mesh=mesh,
        in_specs=placed,
        out_specs=(P("box", "grp", None, None, None), P("grp", None, None)),
        check_vma=False,
    )
```
